32 devices in a mesh: term: 4 (over y, x), sec: 8 (over z, core).
Axes of the slice: x: 2, y: 2, z: 4, core: 2. Of those that a mesh axis runs over, the one named last changes fastest.
Arguments:
- vectors: bfloat16 [1, 512, 256, 256], P(None, 'sec'), may hold values from -6 to 6
- left_env: bfloat16 [4, 16, 256, 256], P('term', 'sec'), may hold values from -0.375 to 0.375
- right_env: bfloat16 [4, 16, 256, 256], P('term', 'sec'), may hold values from -0.375 to 0.375
- left_sector: int32 [8, 64], P('sec'), may hold values from 0 to 1
- right_sector: int32 [8, 64], P('sec'), may hold values from 0 to 1
- tile_count: int32 [8], P('sec'), may hold values from 1 to 64, 384 in all
- departure: int32 [8, 64], P('sec'), may hold values from 0 to 63, each once within a row
- arrival: int32 [8, 64], P('sec'), may hold values from 0 to 63, each once within a row
Outputs:
- sigma: bfloat16 [1, 512, 256, 256], P(None, 'sec', 'term')
The draws below stay inside these ranges and needn't reach their ends.
Inputs may be any that keep to these rules, and one draw needn't show every extreme that they name: `tile_count`: every sec index owns some tile slots that are live; the busiest left owner has all 64 slots live. `departure`: each row is a permutation of the slots. `arrival`: each row is a permutation of the slots.
All inputs are finite; a program needn't handle non-finite values. No bound on the sum of `tile_count` on one device may be relied on, other than what follows from the above.
Results may differ from the reference program's by a relative error of at most 0.015.
Values may be sent and summed in bfloat16 or wider, within the bound.
A program may use at most 128 MiB of HBM per device.

```python
import math
import jax
import jax.numpy as jnp
import numpy as np
from jax import lax

W = 256
SEC_DEV = 2
VECS = 1
TILES_DEV = 64
TILES = 512
SECTORS = 16
TERMS = 4
N_SEC = 8


def plant(values, stream_key, smallest, largest):
    shape = values.shape
    spot = [jax.random.randint(jax.random.fold_in(stream_key, axis), (), 0, shape[axis]) for axis in range(len(shape))]
    values = values.at[tuple(spot)].set(smallest)
    longest = shape.index(max(shape))
    spot[longest] = (spot[longest] + 1) % shape[longest]
    return values.at[tuple(spot)].set(largest)


def shard_levels(rng, extent, split, low, largest):
    def one(dim, parts):
        draws = jax.random.uniform(jax.random.fold_in(jax.random.fold_in(rng, 6), dim), (parts,), jnp.float32, low / len(split), largest / len(split))
        return jnp.repeat(jnp.exp(draws), extent[dim] // parts).reshape((-1,) + (1,) * (len(extent) - dim - 1))

    level = one(*split[0])
    for cut in split[1:]:
        level = level * one(*cut)
    return level


def profile(number_of, total, most, skew):
    portions = [(1 << 20) // math.isqrt(standing ** skew) + 1 for standing in range(2, number_of + 1)]
    rest, given = total - most - (number_of - 1), [1] * (number_of - 1)
    while rest > 0:
        free = [i for i in range(number_of - 1) if given[i] < most]
        pool, remaining = sum([portions[i] for i in free]), rest
        for i in free:
            addition = min(most - given[i], max(1, remaining * portions[i] // pool), rest)
            given[i] = given[i] + addition
            rest = rest - addition
    return np.array([most] + given)


def uneven(stream_key, amount, total, most, skew):
    if amount == 2:
        one = jax.random.randint(stream_key, (), max(1, total - most), min(most, total - 1) + 1)
        return jnp.stack([one, total - one])
    tallies = jnp.asarray(profile(amount, total, most, skew), jnp.int32)
    twos = (amount - 1) // 2
    source_of, receiver = tallies[1:1 + 2 * twos:2], tallies[2:2 + 2 * twos:2]
    room = jnp.minimum(source_of - 1, most - receiver)
    moved = jax.random.randint(jax.random.fold_in(stream_key, 1), (twos,), 0, 1 << 20) % (room + 1)
    tallies = tallies.at[1:1 + 2 * twos:2].set(source_of - moved).at[2:2 + 2 * twos:2].set(receiver + moved)
    return tallies[jax.random.permutation(jax.random.fold_in(stream_key, 2), amount)]


def normal_values(own_key, dims, spread, most, split=(), kind=jnp.bfloat16):
    drawn = spread * jax.random.normal(own_key, dims, jnp.float32)
    if split:
        drawn = drawn * shard_levels(own_key, dims, split, -0.22, 0.18)
    return jnp.clip(drawn, -most, most).astype(kind)


def setup_inputs(seed: int = 0) -> dict:
    splits = jax.random.split(jax.random.key(seed), 9)
    return {
        "vectors": normal_values(splits[0], (VECS, TILES, W, W), 1.0, 6.0, ((1, 8),)),
        "left_env": normal_values(splits[1], (TERMS, SECTORS, W, W), W ** -0.5, 0.375, ((0, 4), (1, 8))),
        "right_env": normal_values(splits[2], (TERMS, SECTORS, W, W), W ** -0.5, 0.375, ((0, 4), (1, 8))),
        "left_sector": plant(jax.random.randint(splits[3], (N_SEC, TILES_DEV), 0, SEC_DEV), jax.random.fold_in(splits[3], 1), 0, SEC_DEV - 1).astype(jnp.int32),
        "right_sector": plant(jax.random.randint(splits[4], (N_SEC, TILES_DEV), 0, SEC_DEV), jax.random.fold_in(splits[4], 1), 0, SEC_DEV - 1).astype(jnp.int32),
        "tile_count": uneven(splits[5], N_SEC, N_SEC * TILES_DEV * 3 // 4, TILES_DEV, 2).astype(jnp.int32),
        "departure": jax.vmap(lambda own: jax.random.permutation(own, TILES_DEV))(jax.random.split(splits[6], N_SEC)).reshape((N_SEC, TILES_DEV)).astype(jnp.int32),
        "arrival": jax.vmap(lambda own: jax.random.permutation(own, TILES_DEV))(jax.random.split(splits[7], N_SEC)).reshape((N_SEC, TILES_DEV)).astype(jnp.int32),
    }


def reference(vectors, left_env, right_env, left_sector, right_sector, tile_count, departure, arrival):
    per_peer = TILES_DEV // N_SEC

    def one_owner(owner):
        arrive = arrival[owner]
        source = arrive // per_peer
        position = owner * per_peer + arrive % per_peer
        left_slot = departure[source, position]
        live = left_slot < tile_count[source]
        left_global = source * SEC_DEV + left_sector[source, left_slot]
        right_global = owner * SEC_DEV + right_sector[owner]
        tiles = vectors[:, source * TILES_DEV + left_slot]
        tiles = jnp.where(live[None, :, None, None], tiles, jnp.zeros_like(tiles))
        left_blocks = left_env[:, left_global]
        right_blocks = right_env[:, right_global]
        applied = jnp.einsum("tkij,vkjl->tvkil", left_blocks.astype(jnp.float32), tiles.astype(jnp.float32)).astype(jnp.bfloat16)
        contrib = jnp.einsum("tvkil,tkml->tvkim", applied.astype(jnp.float32), right_blocks.astype(jnp.float32)).astype(jnp.bfloat16)
        return jnp.sum(contrib.astype(jnp.float32), axis=0).astype(jnp.bfloat16)

    result = lax.map(one_owner, jnp.arange(N_SEC, dtype=jnp.int32))
    result = jnp.transpose(result, (1, 0, 2, 3, 4))
    return result.reshape(VECS, TILES, W, W)
```

```python
import functools

import jax
import jax.numpy as jnp
from jax import lax
from jax.experimental import pallas as pl
from jax.experimental.pallas import tpu as pltpu
from jax.sharding import PartitionSpec as P

MESH = pl.DeviceIdType.MESH


def pick_blocks(table, index):
    picked = jnp.zeros((index.shape[0],) + table.shape[1:], table.dtype)
    for sector in range(table.shape[0]):
        picked = jnp.where((index == sector)[:, None, None], table[sector][None], picked)
    return picked


def place_kernel(tiles, arr, recv, out, sem):
    @pl.loop(0, tiles)
    def _(s):
        pltpu.make_async_copy(recv.at[arr[s]], out.at[s], sem).start()
    pltpu.make_async_copy(recv, out, sem).wait()


def place(tiles, order):
    smem = pl.BlockSpec(memory_space=pltpu.SMEM)
    hbm = pl.BlockSpec(memory_space=pl.ANY)
    return pl.pallas_call(
        functools.partial(place_kernel, tiles.shape[0]),
        out_shape=jax.ShapeDtypeStruct(tiles.shape, tiles.dtype),
        in_specs=[smem, hbm],
        out_specs=hbm,
        scratch_shapes=[pltpu.SemaphoreType.DMA],
    )(order, tiles)


def many_owners(
    vectors, left_env, right_env, left_sector, right_sector, tile_count, departure, arrival
):
    n_sec = lax.axis_size("sec")
    n_vecs = vectors.shape[0]
    tiles_dev = vectors.shape[1]
    width = vectors.shape[3]
    per_peer = tiles_dev // n_sec
    live = (jnp.arange(tiles_dev, dtype=jnp.int32) < tile_count[0]).astype(jnp.bfloat16)
    masked = vectors * live[None, :, None, None]
    left_blocks = pick_blocks(left_env[0], left_sector[0])
    applied = jnp.einsum(
        "kij,vkjl->vkil", left_blocks, masked, preferred_element_type=jnp.float32
    ).astype(jnp.bfloat16)
    outgoing = place(applied[0], departure[0])
    outgoing = outgoing.reshape(n_vecs, n_sec, per_peer, width, width)
    incoming = lax.all_to_all(outgoing, "sec", split_axis=1, concat_axis=1, tiled=True)
    incoming = incoming.reshape(n_vecs, tiles_dev, width, width)
    placed = place(incoming[0], arrival[0])[None]
    right_blocks = pick_blocks(right_env[0], right_sector[0])
    contrib = jnp.einsum(
        "vkil,kml->vkim", placed, right_blocks, preferred_element_type=jnp.float32
    ).astype(jnp.bfloat16)
    return lax.psum_scatter(contrib, "term", scatter_dimension=2, tiled=True)


def exchange_kernel(
    n_sec, n_term, per_peer, rows,
    dep, lsec, cnt, x_hbm, lq, r, sel_src,
    recv,
    x, a, y, out, sel,
    x_sem, own_sem, s_send, s_recv, o_send, o_recv,
):
    me = lax.axis_index("sec")
    load_x = pltpu.make_async_copy(x_hbm, x, x_sem)
    load_x.start()

    def peer(step):
        return lax.rem(me + step, n_sec)

    def sel_copy(to, at):
        return pltpu.make_async_remote_copy(
            src_ref=sel_src.at[to], dst_ref=sel.at[at],
            send_sem=s_send.at[to], recv_sem=s_recv.at[at],
            device_id={"sec": to}, device_id_type=MESH,
        )

    def out_copy(to, at):
        return pltpu.make_async_remote_copy(
            src_ref=out.at[to], dst_ref=recv.at[at],
            send_sem=o_send.at[to], recv_sem=o_recv.at[at],
            device_id={"sec": to}, device_id_type=MESH,
        )

    barrier = pltpu.get_barrier_semaphore()
    for step in range(1, n_sec):
        pl.semaphore_signal(
            barrier, inc=1, device_id={"sec": peer(step)}, device_id_type=MESH
        )
    pl.semaphore_wait(barrier, n_sec - 1)

    for step in range(1, n_sec):
        sel_copy(peer(step), me).start()
    sel[me] = sel_src[me]
    load_x.wait()

    def work(e):
        @pl.loop(0, per_peer)
        def _(j):
            slot = dep[e * per_peer + j]
            p = jnp.dot(lq[lsec[slot]], x[slot], preferred_element_type=jnp.float32)
            p = jnp.where(slot < cnt[0], p, 0.0).astype(jnp.bfloat16)
            for t in range(n_term):
                a[t, pl.ds(pl.multiple_of(j * rows, rows), rows), :] = p[t * rows:(t + 1) * rows]

        width = x.shape[-1]
        for s in range(2):
            total = None
            for t in range(n_term):
                part = lax.dot_general(
                    a[t], r[t, e, s * width:(s + 1) * width, :],
                    (((1,), (1,)), ((), ())), preferred_element_type=jnp.float32,
                )
                total = part if total is None else total + part
            y[s] = total

        @pl.loop(0, per_peer)
        def _(j):
            at = pl.ds(pl.multiple_of(j * rows, rows), rows)
            second = sel[e, pl.ds(j, 1), :] == 1
            out[e, at, :] = jnp.where(second, y[1, at, :], y[0, at, :]).astype(jnp.bfloat16)

    @pl.loop(1, n_sec)
    def _(step):
        e = peer(step)
        sel_copy(e, e).wait_recv()
        work(e)
        out_copy(e, me).start()

    work(me)
    own = pltpu.make_async_copy(out.at[me], recv.at[me], own_sem)
    own.start()
    for step in range(1, n_sec):
        e = peer(step)
        sel_copy(e, me).wait_send()
        out_copy(e, me).wait_send()
        out_copy(e, e).wait_recv()
    own.wait()


def on_device(
    vectors, left_env, right_env, left_sector, right_sector, tile_count, departure, arrival
):
    n_sec = lax.axis_size("sec")
    n_term = lax.axis_size("term")
    tiles = vectors.shape[1]
    width = vectors.shape[3]
    rows = width // n_term
    per_peer = tiles // n_sec
    sectors = left_env.shape[1]

    lq = lax.all_to_all(left_env[0], "term", split_axis=1, concat_axis=1, tiled=True)
    r = lax.all_gather(right_env[0], "sec", axis=0, tiled=True)
    r = lax.all_gather(r, "term", axis=0, tiled=False)
    r = r.reshape(n_term, n_sec, sectors * width, width)
    hits = arrival[0][None, :] == jnp.arange(tiles, dtype=jnp.int32)[:, None]
    chosen = jnp.sum(jnp.where(hits, right_sector[0][None, :], 0), axis=1).astype(jnp.int32)
    chosen = jnp.broadcast_to(chosen.reshape(n_sec, per_peer, 1), (n_sec, per_peer, width))

    vmem = pl.BlockSpec(memory_space=pltpu.VMEM)
    smem = pl.BlockSpec(memory_space=pltpu.SMEM)
    hbm = pl.BlockSpec(memory_space=pl.ANY)
    recv = pl.pallas_call(
        functools.partial(exchange_kernel, n_sec, n_term, per_peer, rows),
        out_shape=jax.ShapeDtypeStruct((n_sec, per_peer * rows, width), jnp.bfloat16),
        in_specs=[smem, smem, smem, hbm, vmem, vmem, vmem],
        out_specs=hbm,
        scratch_shapes=[
            pltpu.VMEM((tiles, width, width), jnp.bfloat16),
            pltpu.VMEM((n_term, per_peer * rows, width), jnp.bfloat16),
            pltpu.VMEM((2, per_peer * rows, width), jnp.float32),
            pltpu.VMEM((n_sec, per_peer * rows, width), jnp.bfloat16),
            pltpu.VMEM((n_sec, per_peer, width), jnp.int32),
            pltpu.SemaphoreType.DMA,
            pltpu.SemaphoreType.DMA,
            pltpu.SemaphoreType.DMA((n_sec,)),
            pltpu.SemaphoreType.DMA((n_sec,)),
            pltpu.SemaphoreType.DMA((n_sec,)),
            pltpu.SemaphoreType.DMA((n_sec,)),
        ],
        compiler_params=pltpu.CompilerParams(
            collective_id=0, has_side_effects=True, vmem_limit_bytes=40 * 1024 * 1024
        ),
    )(departure[0], left_sector[0], tile_count, vectors[0], lq, r, chosen)
    out = place(recv.reshape(tiles, rows, width), arrival[0])
    return out[None]


def solution(mesh):
    in_specs = (
        P(None, "sec", None, None),
        P("term", "sec", None, None),
        P("term", "sec", None, None),
        P("sec", None),
        P("sec", None),
        P("sec"),
        P("sec", None),
        P("sec", None),
    )
    out_specs = P(None, "sec", "term", None)
    body = on_device if mesh.shape["sec"] <= 8 else many_owners
    return jax.shard_map(
        body, mesh=mesh, in_specs=in_specs, out_specs=out_specs, check_vma=False
    )
```

```python
import functools

import jax
import jax.numpy as jnp
from jax import lax
from jax.experimental import pallas as pl
from jax.experimental.pallas import tpu as pltpu
from jax.sharding import PartitionSpec as P

MESH = pl.DeviceIdType.MESH


def pick_blocks(table, index):
    picked = jnp.zeros((index.shape[0],) + table.shape[1:], table.dtype)
    for sector in range(table.shape[0]):
        picked = jnp.where((index == sector)[:, None, None], table[sector][None], picked)
    return picked


def place_kernel(tiles, arr, recv, out, sem):
    @pl.loop(0, tiles)
    def _(s):
        pltpu.make_async_copy(recv.at[arr[s]], out.at[s], sem).start()
    pltpu.make_async_copy(recv, out, sem).wait()


def place(tiles, order):
    smem = pl.BlockSpec(memory_space=pltpu.SMEM)
    hbm = pl.BlockSpec(memory_space=pl.ANY)
    return pl.pallas_call(
        functools.partial(place_kernel, tiles.shape[0]),
        out_shape=jax.ShapeDtypeStruct(tiles.shape, tiles.dtype),
        in_specs=[smem, hbm],
        out_specs=hbm,
        scratch_shapes=[pltpu.SemaphoreType.DMA],
    )(order, tiles)


def many_owners(
    vectors, left_env, right_env, left_sector, right_sector, tile_count, departure, arrival
):
    n_sec = lax.axis_size("sec")
    n_vecs = vectors.shape[0]
    tiles_dev = vectors.shape[1]
    width = vectors.shape[3]
    per_peer = tiles_dev // n_sec
    live = (jnp.arange(tiles_dev, dtype=jnp.int32) < tile_count[0]).astype(jnp.bfloat16)
    masked = vectors * live[None, :, None, None]
    left_blocks = pick_blocks(left_env[0], left_sector[0])
    applied = jnp.einsum(
        "kij,vkjl->vkil", left_blocks, masked, preferred_element_type=jnp.float32
    ).astype(jnp.bfloat16)
    outgoing = place(applied[0], departure[0])
    outgoing = outgoing.reshape(n_vecs, n_sec, per_peer, width, width)
    incoming = lax.all_to_all(outgoing, "sec", split_axis=1, concat_axis=1, tiled=True)
    incoming = incoming.reshape(n_vecs, tiles_dev, width, width)
    placed = place(incoming[0], arrival[0])[None]
    right_blocks = pick_blocks(right_env[0], right_sector[0])
    contrib = jnp.einsum(
        "vkil,kml->vkim", placed, right_blocks, preferred_element_type=jnp.float32
    ).astype(jnp.bfloat16)
    return lax.psum_scatter(contrib, "term", scatter_dimension=2, tiled=True)


def sigma_kernel(
    n_sec, n_term, per_peer, rows, width,
    dep, lsec, cnt, arr, x_hbm, l_src, r_src, sel_src,
    result,
    x, lq, r, a, y, out, recv, sel,
    x_sem, l_send, l_recv, s_send, s_recv, r_send, r_recv, d_recv, o_send, o_recv,
):
    me = lax.axis_index("sec")
    term = lax.axis_index("term")
    z, core = me // 2, me % 2
    tiles = n_sec * per_peer
    load_x = pltpu.make_async_copy(x_hbm, x, x_sem)
    load_x.start()

    chips = (z, z + 1 - 2 * (z % 2), (z + 2) % 4, 3 - z)
    terms = (term, term + 1 - 2 * (term % 2), (term + 2) % 4, 3 - term)
    other = 2 * z + 1 - core

    def to_sec(e):
        return {"sec": e}

    def to_term(t):
        return {"term": t}

    def remote(src, dst, send, recv_sem, device):
        return pltpu.make_async_remote_copy(
            src_ref=src, dst_ref=dst, send_sem=send, recv_sem=recv_sem,
            device_id=device, device_id_type=MESH,
        )

    sent = []

    def start(copy):
        copy.start()
        sent.append(copy)

    def next_send():
        next_send.count += 1
        return r_send.at[next_send.count - 1]

    next_send.count = 0

    def peer(step):
        return lax.rem(me + step, n_sec)

    def block(e):
        return pl.ds(pl.multiple_of(e * per_peer, per_peer), per_peer)

    def quarter(t):
        return pl.ds(pl.multiple_of(t * rows, rows), rows)

    def sel_copy(to, at):
        return remote(sel_src.at[to], sel.at[at], s_send.at[to], s_recv.at[at], to_sec(to))

    def out_copy(to, at):
        return remote(
            out.at[block(to)], recv.at[block(at)], o_send.at[to], o_recv.at[at], to_sec(to)
        )

    def left_copy(to, at):
        return remote(
            l_src.at[:, quarter(to), :], lq.at[:, quarter(at), :],
            l_send.at[to], l_recv.at[at], to_term(to),
        )

    def send_right(t, e, device):
        start(remote(r.at[t, e], r.at[t, e], next_send(), r_recv.at[t, e], device))

    def wait_right(t, e):
        remote(r.at[t, e], r.at[t, e], r_send.at[0], r_recv.at[t, e], to_sec(other)).wait_recv()

    def half_copy(t, e, h, send, device):
        part = r.at[t, e, pl.ds(h * width, width), :]
        return remote(part, part, send, d_recv.at[h, e], device)

    barrier = pltpu.get_barrier_semaphore()
    for step in range(1, n_sec):
        pl.semaphore_signal(barrier, inc=1, device_id=to_sec(peer(step)), device_id_type=MESH)
    for t in terms[1:]:
        pl.semaphore_signal(barrier, inc=1, device_id=to_term(t), device_id_type=MESH)
    r[term, me] = r_src[...]
    lq[:, quarter(term), :] = l_src[:, quarter(term), :]
    sel[me] = sel_src[me]
    pl.semaphore_wait(barrier, n_sec - 1 + n_term - 1)

    for t in terms[1:]:
        left_copy(t, term).start()
    for chip in chips[1:]:
        send_right(term, me, to_sec(2 * chip + core))

    def forward_own(k):
        e = 2 * chips[k] + core
        if k:
            wait_right(term, e)
        for device in (to_term(terms[1]), to_term(terms[2]), to_sec(other)):
            send_right(term, e, device)

    def forward_near(k):
        e = 2 * chips[k] + core
        for h in range(2):
            t = terms[1 + h]
            wait_right(t, e)
            start(half_copy(t, e, h, next_send(), to_term(terms[2 - h])))
            send_right(t, e, to_sec(other))

    def forward_far(k):
        e = 2 * chips[k] + core
        for h in range(2):
            half_copy(terms[3], e, h, r_send.at[0], to_sec(other)).wait_recv()
        send_right(terms[3], e, to_sec(other))

    def left(first, last):
        @pl.loop(first, last, unroll=4)
        def _(p):
            slot = dep[p]
            full = jnp.dot(lq[lsec[slot]], x[slot], preferred_element_type=jnp.float32)
            full = jnp.where(slot < cnt[0], full, 0.0).astype(jnp.bfloat16)
            for t in range(n_term):
                a[t, quarter(p), :] = full[t * rows:(t + 1) * rows]

    def right(e):
        span = pl.ds(pl.multiple_of(e * per_peer * rows, per_peer * rows), per_peer * rows)
        for s in range(2):
            total = None
            for t in range(n_term):
                part = lax.dot_general(
                    a[t, span, :], r[t, e, s * width:(s + 1) * width, :],
                    (((1,), (1,)), ((), ())), preferred_element_type=jnp.float32,
                )
                total = part if total is None else total + part
            y[s] = total

        @pl.loop(0, per_peer, unroll=2)
        def _(i):
            second = sel[e, pl.ds(i, 1), :] == 1
            picked = jnp.where(second, y[1, quarter(i), :], y[0, quarter(i), :])
            out[e * per_peer + i] = picked.astype(jnp.bfloat16)

    def arrived(k):
        e = 2 * chips[k] + 1 - core
        for t in range(n_term):
            wait_right(t, e)

    def stage(k):
        arrived(k)

        @pl.loop(0, 2)
        def _(c):
            e = 2 * chips[k] + c
            sel_copy(e, e).wait_recv()
            right(e)
            out_copy(e, me).start()

    forward_own(0)
    for step in range(1, n_sec):
        sel_copy(peer(step), me).start()
    load_x.wait()
    for t in terms[1:]:
        left_copy(t, t).wait_recv()
    left(0, tiles // 4)
    forward_near(0)
    left(tiles // 4, tiles // 2)
    forward_own(1)
    forward_far(0)
    left(tiles // 2, tiles)
    forward_near(1)
    forward_own(2)
    forward_far(1)
    forward_near(2)
    stage(1)
    forward_own(3)
    forward_far(2)
    forward_near(3)
    stage(2)
    forward_far(3)
    stage(3)
    arrived(0)
    sel_copy(other, other).wait_recv()
    right(other)
    out_copy(other, me).start()
    right(me)
    recv[block(me)] = out[block(me)]

    for step in range(1, n_sec):
        out_copy(peer(step), peer(step)).wait_recv()

    @pl.loop(0, tiles, unroll=4)
    def _(s):
        result[s] = recv[arr[s]]

    for t in terms[1:]:
        left_copy(t, term).wait_send()
    for copy in sent:
        copy.wait_send()
    for step in range(1, n_sec):
        sel_copy(peer(step), me).wait_send()
        out_copy(peer(step), me).wait_send()


def on_device(
    vectors, left_env, right_env, left_sector, right_sector, tile_count, departure, arrival
):
    n_sec = lax.axis_size("sec")
    n_term = lax.axis_size("term")
    tiles = vectors.shape[1]
    width = vectors.shape[3]
    rows = width // n_term
    per_peer = tiles // n_sec
    sectors = left_env.shape[1]

    hits = arrival[0][None, :] == jnp.arange(tiles, dtype=jnp.int32)[:, None]
    chosen = jnp.sum(jnp.where(hits, right_sector[0][None, :], 0), axis=1).astype(jnp.int32)
    chosen = jnp.broadcast_to(chosen.reshape(n_sec, per_peer, 1), (n_sec, per_peer, width))

    vmem = pl.BlockSpec(memory_space=pltpu.VMEM)
    smem = pl.BlockSpec(memory_space=pltpu.SMEM)
    hbm = pl.BlockSpec(memory_space=pl.ANY)
    out = pl.pallas_call(
        functools.partial(sigma_kernel, n_sec, n_term, per_peer, rows, width),
        out_shape=jax.ShapeDtypeStruct((tiles, rows, width), jnp.bfloat16),
        in_specs=[smem, smem, smem, smem, hbm, vmem, vmem, vmem],
        out_specs=vmem,
        scratch_shapes=[
            pltpu.VMEM((tiles, width, width), jnp.bfloat16),
            pltpu.VMEM((sectors, width, width), jnp.bfloat16),
            pltpu.VMEM((n_term, n_sec, sectors * width, width), jnp.bfloat16),
            pltpu.VMEM((n_term, tiles * rows, width), jnp.bfloat16),
            pltpu.VMEM((sectors, per_peer * rows, width), jnp.float32),
            pltpu.VMEM((tiles, rows, width), jnp.bfloat16),
            pltpu.VMEM((tiles, rows, width), jnp.bfloat16),
            pltpu.VMEM((n_sec, per_peer, width), jnp.int32),
            pltpu.SemaphoreType.DMA,
            pltpu.SemaphoreType.DMA((n_term,)),
            pltpu.SemaphoreType.DMA((n_term,)),
            pltpu.SemaphoreType.DMA((n_sec,)),
            pltpu.SemaphoreType.DMA((n_sec,)),
            pltpu.SemaphoreType.DMA((40,)),
            pltpu.SemaphoreType.DMA((n_term, n_sec)),
            pltpu.SemaphoreType.DMA((2, n_sec)),
            pltpu.SemaphoreType.DMA((n_sec,)),
            pltpu.SemaphoreType.DMA((n_sec,)),
        ],
        compiler_params=pltpu.CompilerParams(
            collective_id=0, has_side_effects=True, vmem_limit_bytes=48 * 1024 * 1024
        ),
    )(
        departure[0], left_sector[0], tile_count, arrival[0], vectors[0], left_env[0],
        right_env[0].reshape(sectors * width, width), chosen,
    )
    return out[None]


def solution(mesh):
    in_specs = (
        P(None, "sec", None, None),
        P("term", "sec", None, None),
        P("term", "sec", None, None),
        P("sec", None),
        P("sec", None),
        P("sec"),
        P("sec", None),
        P("sec", None),
    )
    out_specs = P(None, "sec", "term", None)
    small = mesh.shape["sec"] == 8 and mesh.shape["term"] == 4
    body = on_device if small else many_owners
    return jax.shard_map(
        body, mesh=mesh, in_specs=in_specs, out_specs=out_specs, check_vma=False
    )
```

```python
import functools

import jax
import jax.numpy as jnp
from jax import lax
from jax.experimental import pallas as pl
from jax.experimental.pallas import tpu as pltpu
from jax.sharding import PartitionSpec as P

MESH = pl.DeviceIdType.MESH


def pick_blocks(table, index):
    picked = jnp.zeros((index.shape[0],) + table.shape[1:], table.dtype)
    for sector in range(table.shape[0]):
        picked = jnp.where((index == sector)[:, None, None], table[sector][None], picked)
    return picked


def place_kernel(tiles, arr, recv, out, sem):
    @pl.loop(0, tiles)
    def _(s):
        pltpu.make_async_copy(recv.at[arr[s]], out.at[s], sem).start()
    pltpu.make_async_copy(recv, out, sem).wait()


def place(tiles, order):
    smem = pl.BlockSpec(memory_space=pltpu.SMEM)
    hbm = pl.BlockSpec(memory_space=pl.ANY)
    return pl.pallas_call(
        functools.partial(place_kernel, tiles.shape[0]),
        out_shape=jax.ShapeDtypeStruct(tiles.shape, tiles.dtype),
        in_specs=[smem, hbm],
        out_specs=hbm,
        scratch_shapes=[pltpu.SemaphoreType.DMA],
    )(order, tiles)


def many_owners(
    vectors, left_env, right_env, left_sector, right_sector, tile_count, departure, arrival
):
    n_sec = lax.axis_size("sec")
    n_vecs = vectors.shape[0]
    tiles_dev = vectors.shape[1]
    width = vectors.shape[3]
    per_peer = tiles_dev // n_sec
    live = (jnp.arange(tiles_dev, dtype=jnp.int32) < tile_count[0]).astype(jnp.bfloat16)
    masked = vectors * live[None, :, None, None]
    left_blocks = pick_blocks(left_env[0], left_sector[0])
    applied = jnp.einsum(
        "kij,vkjl->vkil", left_blocks, masked, preferred_element_type=jnp.float32
    ).astype(jnp.bfloat16)
    outgoing = place(applied[0], departure[0])
    outgoing = outgoing.reshape(n_vecs, n_sec, per_peer, width, width)
    incoming = lax.all_to_all(outgoing, "sec", split_axis=1, concat_axis=1, tiled=True)
    incoming = incoming.reshape(n_vecs, tiles_dev, width, width)
    placed = place(incoming[0], arrival[0])[None]
    right_blocks = pick_blocks(right_env[0], right_sector[0])
    contrib = jnp.einsum(
        "vkil,kml->vkim", placed, right_blocks, preferred_element_type=jnp.float32
    ).astype(jnp.bfloat16)
    return lax.psum_scatter(contrib, "term", scatter_dimension=2, tiled=True)


def sigma_kernel(
    n_sec, n_term, per_peer, rows, width,
    cnt, dep_hbm, lsec_hbm, rsec_hbm, arr_hbm, x_hbm, l_src, r_src,
    result,
    dep, lsec, arr, arr_row, rsec_row,
    x, lq, r, a, y, out, recv, sel_src, sel,
    in_sem, l_send, l_recv, s_send, s_recv, r_send, r_recv, d_recv, o_send, o_recv,
):
    me = lax.axis_index("sec")
    term = lax.axis_index("term")
    z, core = me // 2, me % 2
    tiles = n_sec * per_peer
    chip_count = n_sec // 2

    chips = (z, 1 + z % 2, (2 + 3 * z) % 5, 3 * (1 - z // 2))
    terms = (term, term + 1 - 2 * (term % 2), (term + 2) % 4, 3 - term)
    other = 2 * z + 1 - core

    def to_sec(e):
        return {"sec": e}

    def to_term(t):
        return {"term": t}

    def remote(src, dst, send, recv_sem, device):
        return pltpu.make_async_remote_copy(
            src_ref=src, dst_ref=dst, send_sem=send, recv_sem=recv_sem,
            device_id=device, device_id_type=MESH,
        )

    sent = []

    def start(copy, when=None):
        sent.append((copy, when))
        if when is None:
            copy.start()
        else:
            pl.when(when)(copy.start)

    def wait_sent(copy, when):
        if when is None:
            copy.wait_send()
        else:
            pl.when(when)(copy.wait_send)

    def next_send():
        next_send.count += 1
        return r_send.at[next_send.count - 1]

    next_send.count = 0

    def peer(step):
        return lax.rem(me + step, n_sec)

    def block(e):
        return pl.ds(pl.multiple_of(e * per_peer, per_peer), per_peer)

    def quarter(t):
        return pl.ds(pl.multiple_of(t * rows, rows), rows)

    def sel_copy(to, at):
        return remote(
            sel_src.at[block(to)], sel.at[block(at)], s_send.at[to], s_recv.at[at], to_sec(to)
        )

    def out_copy(to, at):
        return remote(
            out.at[block(to)], recv.at[block(at)], o_send.at[to], o_recv.at[at], to_sec(to)
        )

    def left_copy(to, at):
        return remote(
            l_src.at[:, quarter(to), :], lq.at[:, quarter(at), :],
            l_send.at[to], l_recv.at[at], to_term(to),
        )

    def send_right(t, e, device, when=None, src=None):
        src = r.at[t, e] if src is None else src
        start(remote(src, r.at[t, e], next_send(), r_recv.at[t, e], device), when)

    def wait_right(t, e):
        remote(r.at[t, e], r.at[t, e], r_send.at[0], r_recv.at[t, e], to_sec(other)).wait_recv()

    def half_copy(t, e, h, send, device):
        part = r.at[t, e, pl.ds(h * width, width), :]
        return remote(part, part, send, d_recv.at[h, e], device)

    barrier = pltpu.get_barrier_semaphore()
    for step in range(1, n_sec):
        pl.semaphore_signal(barrier, inc=1, device_id=to_sec(peer(step)), device_id_type=MESH)
    for t in terms[1:]:
        pl.semaphore_signal(barrier, inc=1, device_id=to_term(t), device_id_type=MESH)
    loads = [
        pltpu.make_async_copy(src, dst, in_sem.at[i])
        for i, (src, dst) in enumerate((
            (arr_hbm, arr_row), (rsec_hbm, rsec_row), (dep_hbm, dep), (lsec_hbm, lsec),
            (arr_hbm, arr), (l_src.at[:, quarter(term), :], lq.at[:, quarter(term), :]),
            (x_hbm, x), (r_src, r.at[term, me]),
        ))
    ]
    for load in loads:
        load.start()
    pl.semaphore_wait(barrier, n_sec - 1 + n_term - 1)

    def forward_own(k):
        e = 2 * chips[k] + core
        src = r_src
        rightward, leftward = z < chip_count - 1, z > 0
        if k:
            src = None
            wait_right(term, e)
            rightward = jnp.logical_and(rightward, chips[k] < z)
            leftward = jnp.logical_and(leftward, chips[k] > z)
        send_right(term, e, to_sec(2 * (z + 1) + core), rightward, src)
        send_right(term, e, to_sec(2 * (z - 1) + core), leftward, src)
        for device in (to_term(terms[1]), to_term(terms[2]), to_sec(other)):
            send_right(term, e, device, None, src)

    def forward_near(k):
        e = 2 * chips[k] + core
        for h in range(2):
            t = terms[1 + h]
            wait_right(t, e)
            start(half_copy(t, e, h, next_send(), to_term(terms[2 - h])))
            send_right(t, e, to_sec(other))

    def forward_far(k):
        e = 2 * chips[k] + core
        for h in range(2):
            half_copy(terms[3], e, h, r_send.at[0], to_sec(other)).wait_recv()
        send_right(terms[3], e, to_sec(other))

    def left(first, last):
        @pl.loop(first, last, unroll=4)
        def _(p):
            slot = dep[0, p]
            full = jnp.dot(lq[lsec[0, slot]], x[slot], preferred_element_type=jnp.float32)
            full = jnp.where(slot < cnt[0], full, 0.0).astype(jnp.bfloat16)
            for t in range(n_term):
                a[t, quarter(p), :] = full[t * rows:(t + 1) * rows]

    def right(e):
        span = pl.ds(pl.multiple_of(e * per_peer * rows, per_peer * rows), per_peer * rows)
        for s in range(2):
            total = None
            for t in range(n_term):
                part = lax.dot_general(
                    a[t, span, :], r[t, e, s * width:(s + 1) * width, :],
                    (((1,), (1,)), ((), ())), preferred_element_type=jnp.float32,
                )
                total = part if total is None else total + part
            y[s] = total

        @pl.loop(0, per_peer, unroll=2)
        def _(i):
            second = sel[pl.ds(e * per_peer + i, 1), :] == 1
            picked = jnp.where(second, y[1, quarter(i), :], y[0, quarter(i), :])
            out[e * per_peer + i] = picked.astype(jnp.bfloat16)

    def arrived(k):
        e = 2 * chips[k] + 1 - core
        for t in range(n_term):
            wait_right(t, e)

    def stage(k):
        arrived(k)

        @pl.loop(0, 2)
        def _(c):
            e = 2 * chips[k] + c
            sel_copy(e, e).wait_recv()
            right(e)
            out_copy(e, me).start()

    forward_own(0)
    for t in terms[1:]:
        left_copy(t, term).start()
    loads[0].wait()
    loads[1].wait()
    position = lax.broadcasted_iota(jnp.int32, (tiles, tiles), 0)
    hits = jnp.where(position == arr_row[...], rsec_row[...], 0)
    sel_src[...] = jnp.broadcast_to(jnp.sum(hits, axis=1, keepdims=True), sel_src.shape)
    for step in range(1, n_sec):
        sel_copy(peer(step), me).start()
    sel[block(me), :] = sel_src[block(me), :]
    for load in loads[2:7]:
        load.wait()
    for t in terms[1:]:
        left_copy(t, t).wait_recv()
    left(0, tiles // 4)
    forward_own(1)
    left(tiles // 4, tiles)
    forward_near(1)
    forward_own(2)
    forward_far(1)
    stage(1)
    forward_near(2)
    forward_own(3)
    forward_far(2)
    stage(2)
    forward_near(3)
    forward_far(3)
    stage(3)
    forward_near(0)
    forward_far(0)
    loads[7].wait()
    arrived(0)
    sel_copy(other, other).wait_recv()
    right(other)
    out_copy(other, me).start()
    right(me)
    recv[block(me)] = out[block(me)]

    for step in range(1, n_sec):
        out_copy(peer(step), peer(step)).wait_recv()

    @pl.loop(0, tiles, unroll=4)
    def _(s):
        result[s] = recv[arr[0, s]]

    for t in terms[1:]:
        left_copy(t, term).wait_send()
    for copy, when in sent:
        wait_sent(copy, when)
    for step in range(1, n_sec):
        sel_copy(peer(step), me).wait_send()
        out_copy(peer(step), me).wait_send()


def on_device(
    vectors, left_env, right_env, left_sector, right_sector, tile_count, departure, arrival
):
    n_sec = lax.axis_size("sec")
    n_term = lax.axis_size("term")
    tiles = vectors.shape[1]
    width = vectors.shape[3]
    rows = width // n_term
    per_peer = tiles // n_sec
    sectors = left_env.shape[1]

    vmem = pl.BlockSpec(memory_space=pltpu.VMEM)
    smem = pl.BlockSpec(memory_space=pltpu.SMEM)
    hbm = pl.BlockSpec(memory_space=pltpu.HBM)
    out = pl.pallas_call(
        functools.partial(sigma_kernel, n_sec, n_term, per_peer, rows, width),
        out_shape=jax.ShapeDtypeStruct((tiles, rows, width), jnp.bfloat16),
        in_specs=[smem] + [hbm] * 7,
        out_specs=vmem,
        scratch_shapes=[
            pltpu.SMEM((1, tiles), jnp.int32),
            pltpu.SMEM((1, tiles), jnp.int32),
            pltpu.SMEM((1, tiles), jnp.int32),
            pltpu.VMEM((1, tiles), jnp.int32),
            pltpu.VMEM((1, tiles), jnp.int32),
            pltpu.VMEM((tiles, width, width), jnp.bfloat16),
            pltpu.VMEM((sectors, width, width), jnp.bfloat16),
            pltpu.VMEM((n_term, n_sec, sectors * width, width), jnp.bfloat16),
            pltpu.VMEM((n_term, tiles * rows, width), jnp.bfloat16),
            pltpu.VMEM((sectors, per_peer * rows, width), jnp.float32),
            pltpu.VMEM((tiles, rows, width), jnp.bfloat16),
            pltpu.VMEM((tiles, rows, width), jnp.bfloat16),
            pltpu.VMEM((tiles, width), jnp.int32),
            pltpu.VMEM((tiles, width), jnp.int32),
            pltpu.SemaphoreType.DMA((8,)),
            pltpu.SemaphoreType.DMA((n_term,)),
            pltpu.SemaphoreType.DMA((n_term,)),
            pltpu.SemaphoreType.DMA((n_sec,)),
            pltpu.SemaphoreType.DMA((n_sec,)),
            pltpu.SemaphoreType.DMA((48,)),
            pltpu.SemaphoreType.DMA((n_term, n_sec)),
            pltpu.SemaphoreType.DMA((2, n_sec)),
            pltpu.SemaphoreType.DMA((n_sec,)),
            pltpu.SemaphoreType.DMA((n_sec,)),
        ],
        compiler_params=pltpu.CompilerParams(
            collective_id=0, has_side_effects=True, vmem_limit_bytes=60 * 1024 * 1024
        ),
    )(
        tile_count, departure, left_sector, right_sector, arrival, vectors[0], left_env[0],
        right_env[0].reshape(sectors * width, width),
    )
    return out[None]


def solution(mesh):
    in_specs = (
        P(None, "sec", None, None),
        P("term", "sec", None, None),
        P("term", "sec", None, None),
        P("sec", None),
        P("sec", None),
        P("sec"),
        P("sec", None),
        P("sec", None),
    )
    out_specs = P(None, "sec", "term", None)
    small = mesh.shape["sec"] == 8 and mesh.shape["term"] == 4
    body = on_device if small else many_owners
    return jax.shard_map(
        body, mesh=mesh, in_specs=in_specs, out_specs=out_specs, check_vma=False
    )
```

```python
import functools

import jax
import jax.numpy as jnp
from jax import lax
from jax.experimental import pallas as pl
from jax.experimental.pallas import tpu as pltpu
from jax.sharding import PartitionSpec as P

MESH = pl.DeviceIdType.MESH


def pick_blocks(table, index):
    picked = jnp.zeros((index.shape[0],) + table.shape[1:], table.dtype)
    for sector in range(table.shape[0]):
        picked = jnp.where((index == sector)[:, None, None], table[sector][None], picked)
    return picked


def place_kernel(tiles, arr, recv, out, sem):
    @pl.loop(0, tiles)
    def _(s):
        pltpu.make_async_copy(recv.at[arr[s]], out.at[s], sem).start()
    pltpu.make_async_copy(recv, out, sem).wait()


def place(tiles, order):
    smem = pl.BlockSpec(memory_space=pltpu.SMEM)
    hbm = pl.BlockSpec(memory_space=pl.ANY)
    return pl.pallas_call(
        functools.partial(place_kernel, tiles.shape[0]),
        out_shape=jax.ShapeDtypeStruct(tiles.shape, tiles.dtype),
        in_specs=[smem, hbm],
        out_specs=hbm,
        scratch_shapes=[pltpu.SemaphoreType.DMA],
    )(order, tiles)


def many_owners(
    vectors, left_env, right_env, left_sector, right_sector, tile_count, departure, arrival
):
    n_sec = lax.axis_size("sec")
    n_vecs = vectors.shape[0]
    tiles_dev = vectors.shape[1]
    width = vectors.shape[3]
    per_peer = tiles_dev // n_sec
    live = (jnp.arange(tiles_dev, dtype=jnp.int32) < tile_count[0]).astype(jnp.bfloat16)
    masked = vectors * live[None, :, None, None]
    left_blocks = pick_blocks(left_env[0], left_sector[0])
    applied = jnp.einsum(
        "kij,vkjl->vkil", left_blocks, masked, preferred_element_type=jnp.float32
    ).astype(jnp.bfloat16)
    outgoing = place(applied[0], departure[0])
    outgoing = outgoing.reshape(n_vecs, n_sec, per_peer, width, width)
    incoming = lax.all_to_all(outgoing, "sec", split_axis=1, concat_axis=1, tiled=True)
    incoming = incoming.reshape(n_vecs, tiles_dev, width, width)
    placed = place(incoming[0], arrival[0])[None]
    right_blocks = pick_blocks(right_env[0], right_sector[0])
    contrib = jnp.einsum(
        "vkil,kml->vkim", placed, right_blocks, preferred_element_type=jnp.float32
    ).astype(jnp.bfloat16)
    return lax.psum_scatter(contrib, "term", scatter_dimension=2, tiled=True)


def sigma_kernel(
    n_sec, n_term, per_peer, rows, width,
    cnt, dep_hbm, lsec_hbm, rsec_hbm, arr_hbm, x_hbm, l_src, r_src,
    result,
    dep, lsec, arr, arr_row, rsec_row,
    x, lq, r, a, y, out, recv, sel_src, sel,
    in_sem, l_send, l_recv, s_send, s_recv, r_send, r_recv, d_recv, o_send, o_recv,
):
    me = lax.axis_index("sec")
    term = lax.axis_index("term")
    z, core = me // 2, me % 2
    tiles = n_sec * per_peer
    chip_count = n_sec // 2

    chips = (z, 1 + z % 2, (2 + 3 * z) % 5, 3 * (1 - z // 2))
    terms = (term, term + 1 - 2 * (term % 2), (term + 2) % 4, 3 - term)
    other = 2 * z + 1 - core

    def to_sec(e):
        return {"sec": e}

    def to_term(t):
        return {"term": t}

    def remote(src, dst, send, recv_sem, device):
        return pltpu.make_async_remote_copy(
            src_ref=src, dst_ref=dst, send_sem=send, recv_sem=recv_sem,
            device_id=device, device_id_type=MESH,
        )

    sent = []

    def start(copy, when=None):
        sent.append((copy, when))
        if when is None:
            copy.start()
        else:
            pl.when(when)(copy.start)

    def wait_sent(copy, when):
        if when is None:
            copy.wait_send()
        else:
            pl.when(when)(copy.wait_send)

    def next_send():
        next_send.count += 1
        return r_send.at[next_send.count - 1]

    next_send.count = 0

    def peer(step):
        return lax.rem(me + step, n_sec)

    def block(e):
        return pl.ds(pl.multiple_of(e * per_peer, per_peer), per_peer)

    def quarter(t):
        return pl.ds(pl.multiple_of(t * rows, rows), rows)

    def sel_copy(to, at):
        return remote(
            sel_src.at[block(to)], sel.at[block(at)], s_send.at[to], s_recv.at[at], to_sec(to)
        )

    def out_copy(to, at):
        return remote(
            out.at[block(to)], recv.at[block(at)], o_send.at[to], o_recv.at[at], to_sec(to)
        )

    def left_copy(to, at):
        return remote(
            l_src.at[:, quarter(to), :], lq.at[:, quarter(at), :],
            l_send.at[to], l_recv.at[at], to_term(to),
        )

    def send_right(t, e, device, when=None, src=None):
        src = r.at[t, e] if src is None else src
        start(remote(src, r.at[t, e], next_send(), r_recv.at[t, e], device), when)

    def wait_right(t, e):
        remote(r.at[t, e], r.at[t, e], r_send.at[0], r_recv.at[t, e], to_sec(other)).wait_recv()

    def half_copy(t, e, h, send, device):
        part = r.at[t, e, pl.ds(h * width, width), :]
        return remote(part, part, send, d_recv.at[h, e], device)

    barrier = pltpu.get_barrier_semaphore()
    for step in range(1, n_sec):
        pl.semaphore_signal(barrier, inc=1, device_id=to_sec(peer(step)), device_id_type=MESH)
    for t in terms[1:]:
        pl.semaphore_signal(barrier, inc=1, device_id=to_term(t), device_id_type=MESH)
    loads = [
        pltpu.make_async_copy(src, dst, in_sem.at[i])
        for i, (src, dst) in enumerate((
            (arr_hbm, arr_row), (rsec_hbm, rsec_row), (dep_hbm, dep), (lsec_hbm, lsec),
            (arr_hbm, arr), (l_src.at[:, quarter(term), :], lq.at[:, quarter(term), :]),
            (x_hbm, x), (r_src, r.at[term, me]),
        ))
    ]
    for load in loads:
        load.start()
    pl.semaphore_wait(barrier, n_sec - 1 + n_term - 1)

    def forward_own(k):
        e = 2 * chips[k] + core
        src = r_src
        rightward, leftward = z < chip_count - 1, z > 0
        if k:
            src = None
            wait_right(term, e)
            rightward = jnp.logical_and(rightward, chips[k] < z)
            leftward = jnp.logical_and(leftward, chips[k] > z)
        send_right(term, e, to_sec(2 * (z + 1) + core), rightward, src)
        send_right(term, e, to_sec(2 * (z - 1) + core), leftward, src)
        for device in (to_term(terms[1]), to_term(terms[2]), to_sec(other)):
            send_right(term, e, device, None, src)

    def forward_near(k):
        e = 2 * chips[k] + core
        for h in range(2):
            t = terms[1 + h]
            wait_right(t, e)
            start(half_copy(t, e, h, next_send(), to_term(terms[2 - h])))
            send_right(t, e, to_sec(other))

    def forward_far(k):
        e = 2 * chips[k] + core
        for h in range(2):
            half_copy(terms[3], e, h, r_send.at[0], to_sec(other)).wait_recv()
        send_right(terms[3], e, to_sec(other))

    def left(first, last):
        @pl.loop(first, last, unroll=4)
        def _(p):
            slot = dep[0, p]
            full = jnp.dot(lq[lsec[0, slot]], x[slot], preferred_element_type=jnp.float32)
            full = jnp.where(slot < cnt[0], full, 0.0).astype(jnp.bfloat16)
            for t in range(n_term):
                a[t, quarter(p), :] = full[t * rows:(t + 1) * rows]

    def right(e):
        span = pl.ds(pl.multiple_of(e * per_peer * rows, per_peer * rows), per_peer * rows)
        for s in range(2):
            total = None
            for t in range(n_term):
                part = lax.dot_general(
                    a[t, span, :], r[t, e, s * width:(s + 1) * width, :],
                    (((1,), (1,)), ((), ())), preferred_element_type=jnp.float32,
                )
                total = part if total is None else total + part
            y[s] = total

        @pl.loop(0, per_peer, unroll=2)
        def _(i):
            second = sel[pl.ds(e * per_peer + i, 1), :] == 1
            picked = jnp.where(second, y[1, quarter(i), :], y[0, quarter(i), :])
            out[e * per_peer + i] = picked.astype(jnp.bfloat16)

    def arrived(k):
        e = 2 * chips[k] + 1 - core
        for t in range(n_term):
            wait_right(t, e)

    def stage(k):
        arrived(k)

        @pl.loop(0, 2)
        def _(c):
            e = 2 * chips[k] + c
            sel_copy(e, e).wait_recv()
            right(e)
            out_copy(e, me).start()

    forward_own(0)
    for t in terms[1:]:
        left_copy(t, term).start()
    loads[0].wait()
    loads[1].wait()
    position = lax.broadcasted_iota(jnp.int32, (tiles, tiles), 0)
    hits = jnp.where(position == arr_row[...], rsec_row[...], 0)
    sel_src[...] = jnp.broadcast_to(jnp.sum(hits, axis=1, keepdims=True), sel_src.shape)
    for step in range(1, n_sec):
        sel_copy(peer(step), me).start()
    sel[block(me), :] = sel_src[block(me), :]
    for load in loads[2:7]:
        load.wait()
    for t in terms[1:]:
        left_copy(t, t).wait_recv()
    left(0, tiles // 4)
    forward_own(1)
    left(tiles // 4, tiles)
    forward_near(1)
    forward_own(2)
    forward_far(1)
    forward_own(3)
    forward_near(2)
    stage(1)
    forward_far(2)
    forward_near(3)
    stage(2)
    forward_far(3)
    forward_near(0)
    stage(3)
    forward_far(0)
    loads[7].wait()
    arrived(0)
    sel_copy(other, other).wait_recv()
    right(other)
    out_copy(other, me).start()
    right(me)
    recv[block(me)] = out[block(me)]

    for step in range(1, n_sec):
        out_copy(peer(step), peer(step)).wait_recv()

    @pl.loop(0, tiles, unroll=4)
    def _(s):
        result[s] = recv[arr[0, s]]

    for t in terms[1:]:
        left_copy(t, term).wait_send()
    for copy, when in sent:
        wait_sent(copy, when)
    for step in range(1, n_sec):
        sel_copy(peer(step), me).wait_send()
        out_copy(peer(step), me).wait_send()


def on_device(
    vectors, left_env, right_env, left_sector, right_sector, tile_count, departure, arrival
):
    n_sec = lax.axis_size("sec")
    n_term = lax.axis_size("term")
    tiles = vectors.shape[1]
    width = vectors.shape[3]
    rows = width // n_term
    per_peer = tiles // n_sec
    sectors = left_env.shape[1]

    vmem = pl.BlockSpec(memory_space=pltpu.VMEM)
    smem = pl.BlockSpec(memory_space=pltpu.SMEM)
    hbm = pl.BlockSpec(memory_space=pltpu.HBM)
    out = pl.pallas_call(
        functools.partial(sigma_kernel, n_sec, n_term, per_peer, rows, width),
        out_shape=jax.ShapeDtypeStruct((tiles, rows, width), jnp.bfloat16),
        in_specs=[smem] + [hbm] * 7,
        out_specs=vmem,
        scratch_shapes=[
            pltpu.SMEM((1, tiles), jnp.int32),
            pltpu.SMEM((1, tiles), jnp.int32),
            pltpu.SMEM((1, tiles), jnp.int32),
            pltpu.VMEM((1, tiles), jnp.int32),
            pltpu.VMEM((1, tiles), jnp.int32),
            pltpu.VMEM((tiles, width, width), jnp.bfloat16),
            pltpu.VMEM((sectors, width, width), jnp.bfloat16),
            pltpu.VMEM((n_term, n_sec, sectors * width, width), jnp.bfloat16),
            pltpu.VMEM((n_term, tiles * rows, width), jnp.bfloat16),
            pltpu.VMEM((sectors, per_peer * rows, width), jnp.float32),
            pltpu.VMEM((tiles, rows, width), jnp.bfloat16),
            pltpu.VMEM((tiles, rows, width), jnp.bfloat16),
            pltpu.VMEM((tiles, width), jnp.int32),
            pltpu.VMEM((tiles, width), jnp.int32),
            pltpu.SemaphoreType.DMA((8,)),
            pltpu.SemaphoreType.DMA((n_term,)),
            pltpu.SemaphoreType.DMA((n_term,)),
            pltpu.SemaphoreType.DMA((n_sec,)),
            pltpu.SemaphoreType.DMA((n_sec,)),
            pltpu.SemaphoreType.DMA((48,)),
            pltpu.SemaphoreType.DMA((n_term, n_sec)),
            pltpu.SemaphoreType.DMA((2, n_sec)),
            pltpu.SemaphoreType.DMA((n_sec,)),
            pltpu.SemaphoreType.DMA((n_sec,)),
        ],
        compiler_params=pltpu.CompilerParams(
            collective_id=0, has_side_effects=True, vmem_limit_bytes=60 * 1024 * 1024
        ),
    )(
        tile_count, departure, left_sector, right_sector, arrival, vectors[0], left_env[0],
        right_env[0].reshape(sectors * width, width),
    )
    return out[None]


def solution(mesh):
    in_specs = (
        P(None, "sec", None, None),
        P("term", "sec", None, None),
        P("term", "sec", None, None),
        P("sec", None),
        P("sec", None),
        P("sec"),
        P("sec", None),
        P("sec", None),
    )
    out_specs = P(None, "sec", "term", None)
    small = mesh.shape["sec"] == 8 and mesh.shape["term"] == 4
    body = on_device if small else many_owners
    return jax.shard_map(
        body, mesh=mesh, in_specs=in_specs, out_specs=out_specs, check_vma=False
    )
```
